32 devices in a mesh: sec: 4 (over y, x), lat: 4 (over z), col: 2 (over core).
Axes of the slice: x: 2, y: 2, z: 4, core: 2. Of those that a mesh axis runs over, the one named last changes fastest.
Arguments:
- physical_state: bfloat16 [32, 64, 5120], P(('sec', 'lat', 'col')), may hold values from -6 to 6
- parallel_lengths: int32 [32], P(('sec', 'lat', 'col')), may hold values from 20 to 5120, as said below
- zonal_mode_assignment: int32 [856], replicated, may hold values from 0 to 640, as said below
- weighted_associated_polynomials: bfloat16 [856, 640, 32], P('lat', None, ('sec', 'col')), may hold values from -1 to 1
- marine_tracer_state: float32 [8, 128, 4096], P(None, ('sec', 'lat', 'col')), may hold values from -6 to 6
- lateral_diffusivity: float32 [128, 4096], P(('sec', 'lat', 'col')), may hold values from 0.015 to 0.15
- depthwise_diffusivity: float32 [128, 4096], P(('sec', 'lat', 'col')), may hold values from 0.02 to 0.2
- water_indicator: int32 [128, 4096], P(('sec', 'lat', 'col')), may hold values 0 or 1
- overlying_parallel: int32 [128], P(('sec', 'lat', 'col')), may hold values from 0 to 31, as said below
- underlying_marine_parallel: int32 [32], P(('sec', 'lat', 'col')), may hold values from 0 to 127, as said below
Outputs:
- harmonic_amounts: float32 [640, 856, 128], P(('sec', 'col'), 'lat')
- ocean_next: float32 [8, 128, 4096], P(None, ('sec', 'lat', 'col'))
The draws below stay inside these ranges and needn't reach their ends.
Inputs may be any that keep to these rules, and one draw needn't show every extreme that they name: `parallel_lengths`: row j holds 20 + 4 * min(max(b + s * j, 0), 1275) points, with s = 42 and one offset b from (5100) // 4 - s * (31) to 0; the first row holds 20 points and the last 5120. `zonal_mode_assignment`: every wavenumber below 640 sits in exactly one slot; the other slots hold 640, meaning empty; slots s with equal s // 214 form a block, at least one block has all its slots taken. overlying_parallel[r] lies between (r // 4 - 1) * 1 and (r // 4 + 2) - 1; some rows reach the lower end and some the upper end. underlying_marine_parallel[j] lies between (j - 1) * 4 and (j + 2) * 4 - 1; some rows reach the lower end and some the upper end.
All inputs are finite; a program needn't handle non-finite values. No bound on the sum of `water_indicator` on one device may be relied on, other than what follows from the above.
Results may differ from the reference program's by a relative error of at most 0.004.
Values may be sent and summed in bfloat16 or wider, within the bound.
A program may use at most 256 MiB of HBM per device.

```python
import math
import jax
import jax.numpy as jnp
from jax import lax

NLON = 5120
M = 640
STRATA = 16
RD = 1
ORD = 4
MARINE_POINTS = 4096
DEPTH_LAYERS = 8
OSTEPS = 4
ROWS = 32
MARINE_LINES = 128
MSLOT = 214
SLOTS = 856
N_LAT = 4
N_COL = 2


def draw_parallel_lengths(key, part):
    equator_index = (NLON - 20) // 4
    stride_rows = (equator_index + ROWS - 1) // (ROWS - 1)
    bottom_stratum = equator_index - stride_rows * (ROWS - 1)
    offset = jax.random.randint(key, (), bottom_stratum, 1)
    latitude = offset + stride_rows * jnp.arange(ROWS, dtype=jnp.int32)
    latitude = jnp.clip(latitude, 0, equator_index)
    return (20 + 4 * latitude).astype(jnp.int32)


def draw_zonal_mode_assignment(key, part):
    key_full, key_order, key_wave = jax.random.split(key, 3)
    full_block = jax.random.randint(key_full, (), 0, SLOTS // MSLOT)
    scores = jax.random.permutation(key_order, SLOTS).astype(jnp.int32)
    owners = jnp.arange(SLOTS, dtype=jnp.int32) // MSLOT
    scores = scores + SLOTS * (owners != full_block).astype(jnp.int32)
    ranking = jnp.argsort(jnp.argsort(scores, stable=True), stable=True).astype(jnp.int32)
    wave_order = jax.random.permutation(key_wave, M).astype(jnp.int32)
    return jnp.where(ranking < M, wave_order[jnp.minimum(ranking, M - 1)], M).astype(jnp.int32)


def neighbour_rows(key, count, own_each, other_each, other_total, every_block):
    index_all = jnp.arange(count, dtype=jnp.int32)
    block_index = index_all // own_each
    base_row = block_index * other_each
    offset = jax.random.randint(key, (count,), -other_each, 2 * other_each)
    chosen = base_row + offset
    first_row = index_all % own_each == 0
    last_row = index_all % own_each == own_each - 1
    if every_block:
        lower_pick = first_row
        upper_pick = last_row & jnp.logical_not(first_row)
    else:
        lower_pick = first_row & (block_index % 2 == 0)
        upper_pick = last_row & (block_index % 4 == 1)
    chosen = jnp.where(lower_pick, base_row - other_each, chosen)
    chosen = jnp.where(upper_pick, base_row + 2 * other_each - 1, chosen)
    return jnp.clip(chosen, 0, other_total - 1).astype(jnp.int32)


def draw_overlying_parallel(key, part):
    return neighbour_rows(key, MARINE_LINES, ORD, RD, ROWS, True)


def draw_underlying_marine_parallel(key, part):
    return neighbour_rows(key, ROWS, RD, ORD, MARINE_LINES, False)


def touch_ends(values, stream_key, least, high):
    shape = values.shape
    place = [jax.random.randint(jax.random.fold_in(stream_key, axis), (), 0, shape[axis]) for axis in range(len(shape))]
    values = values.at[tuple(place)].set(least)
    longest = shape.index(max(shape))
    place[longest] = (place[longest] + 1) % shape[longest]
    return values.at[tuple(place)].set(high)


def block_scale(stream_key, shape, shards, low, top_value):
    def one(position, blocks):
        heights = jax.random.uniform(jax.random.fold_in(jax.random.fold_in(stream_key, 6), position), (blocks,), jnp.float32, low / len(shards), top_value / len(shards))
        return jnp.repeat(jnp.exp(heights), shape[position] // blocks).reshape((-1,) + (1,) * (len(shape) - position - 1))

    level = one(*shards[0])
    for cut in shards[1:]:
        level = level * one(*cut)
    return level


def normal_values(stream_key, extent, scale, most, pieces=(), kind=jnp.bfloat16):
    loudness = block_scale(stream_key, extent, pieces, -0.22, 0.18) if pieces else 1.0
    entries = jax.random.normal(stream_key, extent, jnp.float32) * scale * loudness
    return jnp.minimum(jnp.maximum(entries, -most), most).astype(kind)


def setup_inputs(seed: int = 0) -> dict:
    splits = jax.random.split(jax.random.key(seed), 11)
    physical_state = normal_values(splits[0], (ROWS, 4 * STRATA, NLON), 1.0, 6.0, ((0, 32),))
    parallel_lengths = draw_parallel_lengths(jax.random.fold_in(splits[10], 71), 0)
    zonal_mode_assignment = draw_zonal_mode_assignment(jax.random.fold_in(splits[10], 71), 0)
    weighted_associated_polynomials = normal_values(splits[3], (SLOTS, M, ROWS), ROWS ** -0.5, 1.0, ((0, 4), (2, 8)))
    marine_tracer_state = normal_values(splits[4], (DEPTH_LAYERS, MARINE_LINES, MARINE_POINTS), 1.0, 6.0, ((1, 32),), jnp.float32)
    lateral_diffusivity = jnp.clip(jnp.exp(math.log(0.15) - 2.3025852 * jax.random.uniform(splits[5], (MARINE_LINES, MARINE_POINTS), jnp.float32) ** block_scale(splits[5], (MARINE_LINES, MARINE_POINTS), ((0, 32),), -0.2, 0.2)), 0.015, 0.15)
    depthwise_diffusivity = jnp.clip(jnp.exp(math.log(0.2) - 2.3025851 * jax.random.uniform(splits[6], (MARINE_LINES, MARINE_POINTS), jnp.float32) ** block_scale(splits[6], (MARINE_LINES, MARINE_POINTS), ((0, 32),), -0.2, 0.2)), 0.02, 0.2)
    water_indicator = touch_ends((jax.random.randint(splits[7], (MARINE_LINES, MARINE_POINTS), 0, 5) < 4).astype(jnp.int32), jax.random.fold_in(splits[7], 1), 0, 1)
    overlying_parallel = draw_overlying_parallel(jax.random.fold_in(splits[10], 71), 0)
    underlying_marine_parallel = draw_underlying_marine_parallel(jax.random.fold_in(splits[10], 71), 0)
    return dict(physical_state=physical_state, parallel_lengths=parallel_lengths, zonal_mode_assignment=zonal_mode_assignment, weighted_associated_polynomials=weighted_associated_polynomials, marine_tracer_state=marine_tracer_state, lateral_diffusivity=lateral_diffusivity, depthwise_diffusivity=depthwise_diffusivity, water_indicator=water_indicator, overlying_parallel=overlying_parallel, underlying_marine_parallel=underlying_marine_parallel)


two_pi = 6.283185307179586
thermal_transfer_factor = 0.8
force_coef = 0.1

def fourier_table(row_points, wave_count, grid_width):
    wave_index = jnp.arange(wave_count, dtype=jnp.int32)
    positions = jnp.arange(grid_width, dtype=jnp.int32)
    points_float = row_points.astype(jnp.float32)
    angle_unit = jnp.float32(two_pi) / points_float
    residue = wave_index[:, None] * positions[None, :] % row_points
    angle = residue.astype(jnp.float32) * angle_unit
    inside = (positions[None, :] < row_points) & (wave_index[:, None] < row_points // 2)
    norm_factor = 1.0 / jnp.sqrt(points_float)
    real_part = jnp.where(inside, jnp.cos(angle) * norm_factor, 0.0)
    imag_part = jnp.where(inside, -jnp.sin(angle) * norm_factor, 0.0)
    return jnp.stack([real_part, imag_part]).astype(jnp.bfloat16)

def transform_order(row_total, lat_count, col_count, rows_each):
    index_all = jnp.arange(row_total, dtype=jnp.int32)
    group_rows = lat_count * rows_each
    group_id = index_all // group_rows
    within = index_all % group_rows
    return ((group_id // col_count * lat_count + within // rows_each) * col_count + group_id % col_count) * rows_each + within % rows_each

def advance_coupled_model(bordered_array, meridian_exchange_factor, zonal_exchange_factor, depthwise_exchange_factor, boundary_warming_term):
    centre = bordered_array[:, 1:-1]
    meridional = meridian_exchange_factor[1:] * (bordered_array[:, 2:] - centre) - meridian_exchange_factor[:-1] * (centre - bordered_array[:, :-2])
    east_flux = zonal_exchange_factor * (jnp.roll(centre, -1, axis=2) - centre)
    zonal_div = east_flux - jnp.roll(east_flux, 1, axis=2)
    vertical_flux = depthwise_exchange_factor * (centre[1:] - centre[:-1])
    zero_layer = jnp.zeros_like(vertical_flux[:1])
    vertical = jnp.concatenate([vertical_flux, zero_layer], 0) - jnp.concatenate([zero_layer, vertical_flux], 0)
    forced = jnp.concatenate([boundary_warming_term[None], jnp.zeros_like(centre[1:])], 0)
    return centre + meridional + zonal_div + vertical + forced

def reference(physical_state, parallel_lengths, zonal_mode_assignment, weighted_associated_polynomials, marine_tracer_state, lateral_diffusivity, depthwise_diffusivity, water_indicator, overlying_parallel, underlying_marine_parallel):
    vector_width = 8 * STRATA

    def row_transform(row_pair):
        fourier_matrix = fourier_table(row_pair[1], M, NLON).astype(jnp.float32)
        result = jnp.einsum('pmi,vi->mpv', fourier_matrix, row_pair[0].astype(jnp.float32), precision=lax.Precision.HIGHEST)
        return result.reshape(M, vector_width).astype(jnp.bfloat16)
    fourier = lax.map(row_transform, (physical_state, parallel_lengths))
    row_order = transform_order(ROWS, N_LAT, N_COL, RD)
    sorted_rows = jnp.take(fourier, row_order, axis=0)
    degrees = jnp.arange(M, dtype=jnp.int32)

    def slot_block(block_index):
        waves_here = lax.dynamic_slice_in_dim(zonal_mode_assignment, block_index * MSLOT, MSLOT)
        chosen = jnp.take(sorted_rows, jnp.clip(waves_here, 0, M - 1), axis=1).astype(jnp.float32)
        values = lax.dynamic_slice_in_dim(weighted_associated_polynomials, block_index * MSLOT, MSLOT, 0).astype(jnp.float32)
        summed = jnp.einsum('snq,qsv->nsv', values, chosen, precision=lax.Precision.HIGHEST)
        return jnp.where(degrees[:, None, None] >= waves_here[None, :, None], summed, 0.0)
    blocks = lax.map(slot_block, jnp.arange(N_LAT, dtype=jnp.int32))
    harmonic_amounts = jnp.transpose(blocks, (1, 0, 2, 3)).reshape(M, SLOTS, vector_width)
    skin_warmth_parallels = jnp.take(marine_tracer_state[0], underlying_marine_parallel, axis=0)
    grid_points = jnp.arange(NLON, dtype=jnp.int32)
    sea_column_index = jnp.minimum(grid_points[None, :] * MARINE_POINTS // parallel_lengths[:, None], MARINE_POINTS - 1)
    skin_warmth_mapped_upward = jnp.take_along_axis(skin_warmth_parallels, sea_column_index, axis=1)
    bottom_stratum = STRATA - 1
    zonal_wind = physical_state[:, bottom_stratum].astype(jnp.float32)
    meridional_wind = physical_state[:, STRATA + bottom_stratum].astype(jnp.float32)
    lowest_layer_warmth = physical_state[:, 2 * STRATA + bottom_stratum].astype(jnp.float32)
    breeze_speed = jnp.sqrt(zonal_wind * zonal_wind + meridional_wind * meridional_wind + 1.0)
    boundary_energy_exchange = thermal_transfer_factor * breeze_speed * (skin_warmth_mapped_upward - lowest_layer_warmth)
    ocean_points = jnp.arange(MARINE_POINTS, dtype=jnp.int32)
    grid_column = ocean_points[None, :] * parallel_lengths[:, None] // MARINE_POINTS
    flux_rows = jnp.take_along_axis(boundary_energy_exchange, grid_column, axis=1)
    forcing = jnp.take(flux_rows, overlying_parallel, axis=0)
    water_share = water_indicator.astype(jnp.float32)
    sea_pad = jnp.pad(water_share, ((1, 1), (0, 0)))
    kappa_pad = jnp.pad(lateral_diffusivity, ((1, 1), (0, 0)))
    meridian_exchange_factor = 0.5 * (kappa_pad[:-1] + kappa_pad[1:]) * sea_pad[:-1] * sea_pad[1:]
    zonal_exchange_factor = 0.5 * (lateral_diffusivity + jnp.roll(lateral_diffusivity, -1, axis=1)) * water_share * jnp.roll(water_share, -1, axis=1)
    depthwise_exchange_factor = depthwise_diffusivity * water_share
    boundary_warming_term = force_coef * water_share * forcing
    thermal_state = marine_tracer_state
    for iteration in range(OSTEPS):
        bordered_array = jnp.pad(thermal_state, ((0, 0), (1, 1), (0, 0)))
        thermal_state = advance_coupled_model(bordered_array, meridian_exchange_factor, zonal_exchange_factor, depthwise_exchange_factor, boundary_warming_term)
    return (harmonic_amounts, thermal_state)
```

```python
import functools

import jax
import jax.numpy as jnp
from jax import lax
from jax.experimental import pallas as pl
from jax.experimental.pallas import tpu as pltpu
from jax.sharding import PartitionSpec as P

OSTEPS = 4
LOW = 8
CHUNK = 256
SLOT_PAD = 16

two_pi = 6.283185307179586
thermal_transfer_factor = 0.8
force_coef = 0.1

GROUP = ("sec", "col")
LINE = ("sec", "lat", "col")


def angle_tables(points, wave_count, grid_width):
    low = jnp.arange(LOW, dtype=jnp.float32)
    mid = jnp.arange(CHUNK // LOW, dtype=jnp.float32) * LOW
    high = jnp.arange(grid_width // CHUNK, dtype=jnp.float32) * CHUNK
    place = jnp.concatenate([low, mid, high])
    count = points.astype(jnp.float32)
    product = place[:, None] * jnp.arange(wave_count, dtype=jnp.float32)[None, :]
    residue = product - jnp.round(product / count) * count
    angle = residue * (jnp.float32(two_pi) / count)
    scale = jnp.where(jnp.arange(place.shape[0]) >= LOW + CHUNK // LOW, 1.0 / jnp.sqrt(count), 1.0)
    return jnp.stack([jnp.cos(angle), -jnp.sin(angle)]) * scale[None, :, None]


def fourier_kernel(points_ref, table_ref, slots_ref, x_ref, out_ref, base_ref, acc_ref):
    points = points_ref[0]
    waves = table_ref.shape[2]
    fields = x_ref.shape[0]
    chunks = x_ref.shape[1] // CHUNK
    low_c, low_s = table_ref[0, :LOW], table_ref[1, :LOW]
    for b in range(CHUNK // LOW):
        mid_c = table_ref[0, LOW + b : LOW + b + 1]
        mid_s = table_ref[1, LOW + b : LOW + b + 1]
        base_ref[0, b * LOW : (b + 1) * LOW] = low_c * mid_c - low_s * mid_s
        base_ref[1, b * LOW : (b + 1) * LOW] = low_c * mid_s + low_s * mid_c
    acc_ref[...] = jnp.zeros_like(acc_ref)
    top = LOW + CHUNK // LOW

    @pl.loop(0, chunks)
    def _(a):
        start = pl.multiple_of(a * CHUNK, CHUNK)
        position = start + lax.broadcasted_iota(jnp.int32, (fields, CHUNK), 1)
        block = x_ref[:, pl.ds(start, CHUNK)].astype(jnp.float32)
        block = jnp.where(position < points, block, 0.0).astype(jnp.bfloat16)
        high_c = table_ref[0, pl.ds(top + a, 1)]
        high_s = table_ref[1, pl.ds(top + a, 1)]
        for w in range(0, waves, 128):
            cut = slice(w, w + 128)
            base_c, base_s = base_ref[0, :, cut], base_ref[1, :, cut]
            turn_c, turn_s = high_c[:, cut], high_s[:, cut]
            real = (base_c * turn_c - base_s * turn_s).astype(jnp.bfloat16)
            imag = (base_c * turn_s + base_s * turn_c).astype(jnp.bfloat16)
            both = jnp.concatenate([real, imag], axis=1)
            part = jnp.dot(block, both, preferred_element_type=jnp.float32)
            acc_ref[:fields, cut] += part[:, :128]
            acc_ref[fields:, cut] += part[:, 128:]

    wave = lax.broadcasted_iota(jnp.int32, acc_ref.shape, 1)
    coefs = jnp.where(wave < points // 2, acc_ref[...], 0.0).astype(jnp.bfloat16)
    rows = 112 if slots_ref.shape[0] % 112 == 0 else slots_ref.shape[0] // 8

    @pl.loop(0, slots_ref.shape[0] // rows)
    def _(b):
        start = pl.multiple_of(b * rows, 16)
        held = slots_ref[pl.ds(start, rows)]
        pick = held == lax.broadcasted_iota(jnp.int32, (rows, waves), 1)
        pick = jnp.where(pick, 1.0, 0.0).astype(jnp.bfloat16)
        out_ref[pl.ds(start, rows)] = lax.dot_general(
            pick, coefs, (((1,), (1,)), ((), ())), preferred_element_type=jnp.float32
        ).astype(jnp.bfloat16)


def fourier_slots(state, points, slots):
    fields, width = state.shape
    waves = slots[1]
    table = angle_tables(points[0], waves, width)
    return pl.pallas_call(
        fourier_kernel,
        out_shape=jax.ShapeDtypeStruct((slots[0].shape[0], 2 * fields), jnp.bfloat16),
        in_specs=[
            pl.BlockSpec(memory_space=pltpu.SMEM),
            pl.BlockSpec(memory_space=pltpu.VMEM),
            pl.BlockSpec(memory_space=pltpu.VMEM),
            pl.BlockSpec(memory_space=pltpu.VMEM),
        ],
        out_specs=pl.BlockSpec(memory_space=pltpu.VMEM),
        scratch_shapes=[
            pltpu.VMEM((2, CHUNK, waves), jnp.float32),
            pltpu.VMEM((2 * fields, waves), jnp.float32),
        ],
        compiler_params=pltpu.CompilerParams(vmem_limit_bytes=32 * 2**20),
        cost_estimate=pl.CostEstimate(
            flops=4 * fields * waves * width, bytes_accessed=4 * 2**20, transcendentals=0
        ),
    )(points, table, slots[0], state)


def legendre_kernel(degree_ref, slots_ref, weight_ref, coef_ref, out_ref):
    rows, pair, width = coef_ref.shape
    degrees = out_ref.shape[1]
    first = degree_ref[0]
    for half in range(pair // 8):
        cut = slice(half * 8, half * 8 + 8)
        values = weight_ref[:, cut, :].astype(jnp.float32).reshape(rows * 8, weight_ref.shape[2])
        values = values.T[:degrees]
        lane_slot = lax.broadcasted_iota(jnp.int32, (degrees, rows * 8), 1) % 8
        coefs = coef_ref[:, cut, :].astype(jnp.float32).reshape(rows * 8, width).astype(jnp.bfloat16)
        degree = first + lax.broadcasted_iota(jnp.int32, (degrees, rows * 8), 0)
        for s in range(8):
            wave = slots_ref[pl.program_id(0) * pair + half * 8 + s]
            keep = (lane_slot == s) & (degree >= wave)
            left = jnp.where(keep, values, 0.0).astype(jnp.bfloat16)
            out_ref[half * 8 + s] = jnp.dot(left, coefs, preferred_element_type=jnp.float32)


def legendre(weights, coefs, slots, first_degree, slot_count, degrees):
    rows, padded, width = coefs.shape
    return pl.pallas_call(
        legendre_kernel,
        grid=(padded // SLOT_PAD,),
        out_shape=jax.ShapeDtypeStruct((slot_count, degrees, width), jnp.float32),
        in_specs=[
            pl.BlockSpec(memory_space=pltpu.SMEM),
            pl.BlockSpec(memory_space=pltpu.SMEM),
            pl.BlockSpec((rows, SLOT_PAD, weights.shape[2]), lambda i: (0, i, 0)),
            pl.BlockSpec((rows, SLOT_PAD, width), lambda i: (0, i, 0)),
        ],
        out_specs=pl.BlockSpec((SLOT_PAD, degrees, width), lambda i: (i, 0, 0)),
        compiler_params=pltpu.CompilerParams(vmem_limit_bytes=40 * 2**20),
        cost_estimate=pl.CostEstimate(
            flops=2 * rows * padded * width * degrees * 8,
            bytes_accessed=4 * slot_count * degrees * width + 4 * rows * padded * width,
            transcendentals=0,
        ),
    )(first_degree, slots, weights, coefs)


def split_two(values):
    top = lax.reduce_precision(values, 8, 7)
    return [top.astype(jnp.bfloat16), (values - top).astype(jnp.bfloat16)]


def pick_points(arrays, index):
    length = arrays[0].shape[0]
    tiles = -(-length // 128)
    matrix = jnp.stack(arrays).reshape(len(arrays), tiles, 128)
    chosen = (jnp.arange(tiles, dtype=jnp.int32)[:, None] == index[None, :] // 128).astype(jnp.bfloat16)
    spread = jnp.einsum("kta,tx->kax", matrix, chosen, preferred_element_type=jnp.float32)
    lane = jnp.arange(128, dtype=jnp.int32)[:, None] == index[None, :] % 128
    return jnp.where(lane[None], spread, 0.0).sum(axis=1)


def shifted(array, axis, count, step):
    pairs = [(i, i + step) for i in range(count) if 0 <= i + step < count]
    return lax.ppermute(array, axis, pairs)


def advance_coupled_model(
    bordered_array,
    meridian_exchange_factor,
    zonal_exchange_factor,
    depthwise_exchange_factor,
    boundary_warming_term,
):
    centre = bordered_array[:, 1:-1]
    meridional = meridian_exchange_factor[1:] * (
        bordered_array[:, 2:] - centre
    ) - meridian_exchange_factor[:-1] * (centre - bordered_array[:, :-2])
    east_flux = zonal_exchange_factor * (jnp.roll(centre, -1, axis=2) - centre)
    zonal_div = east_flux - jnp.roll(east_flux, 1, axis=2)
    vertical_flux = depthwise_exchange_factor * (centre[1:] - centre[:-1])
    zero_layer = jnp.zeros_like(vertical_flux[:1])
    vertical = jnp.concatenate([vertical_flux, zero_layer], 0) - jnp.concatenate(
        [zero_layer, vertical_flux], 0
    )
    forced = jnp.concatenate([boundary_warming_term[None], jnp.zeros_like(centre[1:])], 0)
    return centre + meridional + zonal_div + vertical + forced


def body(
    physical_state,
    parallel_lengths,
    zonal_mode_assignment,
    weighted_associated_polynomials,
    marine_tracer_state,
    lateral_diffusivity,
    depthwise_diffusivity,
    water_indicator,
    overlying_parallel,
    underlying_marine_parallel,
):
    lat_count = lax.axis_size("lat")
    groups = lax.axis_size("sec") * lax.axis_size("col")
    devices = groups * lat_count
    grid_width = physical_state.shape[2]
    strata = physical_state.shape[1] // 4
    slot_count, wave_count, row_count = weighted_associated_polynomials.shape
    block_degrees = wave_count // groups
    padded = -(-slot_count // SLOT_PAD) * SLOT_PAD
    linear_index = (
        lax.axis_index("sec") * lat_count + lax.axis_index("lat")
    ) * lax.axis_size("col") + lax.axis_index("col")
    group_index = lax.axis_index("sec") * lax.axis_size("col") + lax.axis_index("col")
    points = parallel_lengths[0]

    rows = marine_tracer_state.shape[1]
    span = marine_tracer_state.shape[2]
    layers = marine_tracer_state.shape[0]
    sea = water_indicator.astype(jnp.float32)
    relative = (overlying_parallel - linear_index).astype(jnp.float32)
    payload = jnp.concatenate(
        [
            marine_tracer_state,
            lateral_diffusivity[None],
            depthwise_diffusivity[None],
            sea[None],
            jnp.broadcast_to(relative[:, None], (rows, span))[None],
        ],
        axis=0,
    )
    before = shifted(payload, LINE, devices, 1)
    after = shifted(payload, LINE, devices, -1)

    send = weighted_associated_polynomials.reshape(slot_count, groups, block_degrees, row_count)
    send = jnp.transpose(send, (1, 3, 0, 2))
    send = jnp.pad(send, ((0, 0), (0, 0), (0, padded - slot_count), (0, 128 - block_degrees)))
    weights = lax.all_to_all(send, GROUP, split_axis=0, concat_axis=0, tiled=True)
    weights = weights.reshape(groups * row_count, padded, 128)

    slots = zonal_mode_assignment.reshape(lat_count, slot_count)
    slots = jnp.pad(slots, ((0, 0), (0, padded - slot_count)), constant_values=wave_count)
    outgoing = fourier_slots(
        physical_state[0], parallel_lengths, (slots.reshape(-1, 1), wave_count)
    )
    outgoing = outgoing.reshape(lat_count, padded, outgoing.shape[1])
    incoming = lax.all_to_all(outgoing, "lat", split_axis=0, concat_axis=0, tiled=True)
    coefs = lax.all_gather(incoming, GROUP, axis=0, tiled=True)

    surface = jnp.concatenate([before[0], marine_tracer_state[0], after[0]], axis=0)
    under = underlying_marine_parallel[0] - (linear_index - 1) * rows
    skin = jnp.where(jnp.arange(3 * rows)[:, None] == under, surface, 0.0).sum(axis=0)
    ocean_points = jnp.arange(span, dtype=jnp.int32)
    column = ocean_points * points // span
    sea_column = jnp.minimum(column * span // points, span - 1)
    skin_hi, skin_lo = split_two(skin)
    mapped = pick_points([skin_hi, skin_lo], sea_column)
    bottom = strata - 1
    zonal_wind = physical_state[0, bottom].astype(jnp.float32)
    meridional_wind = physical_state[0, strata + bottom].astype(jnp.float32)
    speed = thermal_transfer_factor * jnp.sqrt(
        zonal_wind * zonal_wind + meridional_wind * meridional_wind + 1.0
    )
    speed_hi, speed_lo = split_two(speed)
    picked = pick_points([speed_hi, speed_lo, physical_state[0, 2 * strata + bottom]], column)
    flux = (picked[0] + picked[1]) * (mapped[0] + mapped[1] - picked[2])
    flux_near = {
        step: shifted(flux, LINE, devices, -step) if step else flux for step in (-2, -1, 0, 1, 2)
    }

    whole = jnp.concatenate([before, payload, after], axis=1)
    thermal = whole[:layers]
    kappa, depth, sea, relative = (whole[layers + k] for k in range(4))
    owner = jnp.arange(3 * rows, dtype=jnp.int32)[:, None] // rows - 1
    target = relative + owner.astype(jnp.float32)
    forcing = jnp.zeros_like(sea)
    for step, row in flux_near.items():
        forcing = jnp.where(target == step, row[None], forcing)
    source = force_coef * sea * forcing
    depthwise = depth * sea
    faces = 0.5 * (kappa[:-1] + kappa[1:]) * sea[:-1] * sea[1:]
    east = 0.5 * (kappa + jnp.roll(kappa, -1, axis=1)) * sea * jnp.roll(sea, -1, axis=1)
    total = 3 * rows
    for iteration in range(OSTEPS):
        a, b = iteration + 1, total - iteration - 1
        thermal = advance_coupled_model(
            thermal, faces[a - 1 : b], east[a:b], depthwise[a:b], source[a:b]
        )

    own_waves = lax.dynamic_slice_in_dim(
        slots.reshape(-1), lax.axis_index("lat") * padded, padded
    )
    first_degree = jnp.reshape(group_index * block_degrees, (1,)).astype(jnp.int32)
    harmonic = legendre(weights, coefs, own_waves, first_degree, slot_count, block_degrees)
    return (jnp.transpose(harmonic, (1, 0, 2)), thermal)


def solution(mesh):
    return jax.shard_map(
        body,
        mesh=mesh,
        in_specs=(
            P(LINE, None, None),
            P(LINE),
            P(),
            P("lat", None, GROUP),
            P(None, LINE, None),
            P(LINE, None),
            P(LINE, None),
            P(LINE, None),
            P(LINE),
            P(LINE),
        ),
        out_specs=(P(GROUP, "lat", None), P(None, LINE, None)),
        check_vma=False,
    )
```

```python
import functools

import jax
import jax.numpy as jnp
from jax import lax
from jax.experimental import pallas as pl
from jax.experimental.pallas import tpu as pltpu
from jax.sharding import PartitionSpec as P

OSTEPS = 4
LOW = 8
CHUNK = 256
SLOT_PAD = 16

two_pi = 6.283185307179586
thermal_transfer_factor = 0.8
force_coef = 0.1

GROUP = ("sec", "col")
LINE = ("sec", "lat", "col")


def angle_tables(points, wave_count, grid_width):
    low = jnp.arange(LOW, dtype=jnp.float32)
    mid = jnp.arange(CHUNK // LOW, dtype=jnp.float32) * LOW
    high = jnp.arange(grid_width // CHUNK, dtype=jnp.float32) * CHUNK
    place = jnp.concatenate([low, mid, high])
    count = points.astype(jnp.float32)
    product = place[:, None] * jnp.arange(wave_count, dtype=jnp.float32)[None, :]
    residue = product - jnp.round(product / count) * count
    angle = residue * (jnp.float32(two_pi) / count)
    scale = jnp.where(jnp.arange(place.shape[0]) >= LOW + CHUNK // LOW, 1.0 / jnp.sqrt(count), 1.0)
    return jnp.stack([jnp.cos(angle), -jnp.sin(angle)]) * scale[None, :, None]


MESH = pl.DeviceIdType.MESH


def place_of(index, lat_count, col_count):
    return {
        "sec": index // (lat_count * col_count),
        "lat": index // col_count % lat_count,
        "col": index % col_count,
    }


def exchange_kernel(
    sizes,
    points_ref,
    table_ref,
    slots_ref,
    x_ref,
    weight_ref,
    *refs,
):
    sec_count, lat_count, col_count = sizes
    halo = refs[:5]
    coef_out, weight_out = refs[5:7]
    before, after = refs[7:12], refs[12:17]
    (base_ref, acc_ref, mine_ref, local_sem, weight_send, weight_recv, halo_send, halo_recv,
     lat_send, lat_recv, group_send, group_recv) = refs[17:]
    groups = sec_count * col_count
    devices = groups * lat_count
    sec, lat, col = (lax.axis_index(name) for name in LINE)
    group = sec * col_count + col
    line = (sec * lat_count + lat) * col_count + col
    following = place_of((line + 1) % devices, lat_count, col_count)
    previous = place_of((line + devices - 1) % devices, lat_count, col_count)

    def group_place(step):
        other = (group + step) % groups
        return other, {"sec": other // col_count, "lat": lat, "col": other % col_count}

    def lat_place(step):
        other = (lat + step) % lat_count
        return other, {"sec": sec, "lat": other, "col": col}

    barrier = pltpu.get_barrier_semaphore()
    for place in (following, previous):
        pl.semaphore_signal(barrier, inc=1, device_id=place, device_id_type=MESH)

    @pl.loop(1, groups)
    def _(step):
        pl.semaphore_signal(barrier, inc=1, device_id=group_place(step)[1], device_id_type=MESH)

    @pl.loop(1, lat_count)
    def _(step):
        pl.semaphore_signal(barrier, inc=1, device_id=lat_place(step)[1], device_id_type=MESH)

    pl.semaphore_wait(barrier, groups + lat_count)

    def weight_copy(step):
        other, place = group_place(step)
        return pltpu.make_async_remote_copy(
            src_ref=weight_ref.at[other],
            dst_ref=weight_out.at[group],
            send_sem=weight_send.at[step],
            recv_sem=weight_recv.at[step],
            device_id=place,
            device_id_type=MESH,
        )

    def halo_copies():
        return [
            pltpu.make_async_remote_copy(
                src_ref=halo[k],
                dst_ref=target[k],
                send_sem=halo_send.at[side, k],
                recv_sem=halo_recv.at[side, k],
                device_id=place,
                device_id_type=MESH,
            )
            for k in range(5)
            for side, (target, place) in enumerate(((before, following), (after, previous)))
        ]

    def lat_copy(step):
        other, place = lat_place(step)
        return pltpu.make_async_remote_copy(
            src_ref=mine_ref.at[other],
            dst_ref=coef_out.at[group, lat],
            send_sem=lat_send.at[step],
            recv_sem=lat_recv.at[step],
            device_id=place,
            device_id_type=MESH,
        )

    def group_copy(step):
        return pltpu.make_async_remote_copy(
            src_ref=coef_out.at[group],
            dst_ref=coef_out.at[group],
            send_sem=group_send.at[step],
            recv_sem=group_recv.at[step],
            device_id=group_place(step)[1],
            device_id_type=MESH,
        )

    for copy in halo_copies():
        copy.start()
    own_weights = pltpu.make_async_copy(weight_ref.at[group], weight_out.at[group], local_sem.at[0])
    own_weights.start()

    @pl.loop(1, groups)
    def _(step):
        weight_copy(step).start()

    points = points_ref[0]
    waves = table_ref.shape[2]
    fields = x_ref.shape[0]
    chunks = x_ref.shape[1] // CHUNK
    low_c, low_s = table_ref[0, :LOW], table_ref[1, :LOW]
    for b in range(CHUNK // LOW):
        mid_c = table_ref[0, LOW + b : LOW + b + 1]
        mid_s = table_ref[1, LOW + b : LOW + b + 1]
        base_ref[0, b * LOW : (b + 1) * LOW] = low_c * mid_c - low_s * mid_s
        base_ref[1, b * LOW : (b + 1) * LOW] = low_c * mid_s + low_s * mid_c
    acc_ref[...] = jnp.zeros_like(acc_ref)
    top = LOW + CHUNK // LOW

    @pl.loop(0, chunks)
    def _(a):
        start = pl.multiple_of(a * CHUNK, CHUNK)
        position = start + lax.broadcasted_iota(jnp.int32, (fields, CHUNK), 1)
        block = x_ref[:, pl.ds(start, CHUNK)].astype(jnp.float32)
        block = jnp.where(position < points, block, 0.0).astype(jnp.bfloat16)
        high_c = table_ref[0, pl.ds(top + a, 1)]
        high_s = table_ref[1, pl.ds(top + a, 1)]
        for w in range(0, waves, 128):
            cut = slice(w, w + 128)
            base_c, base_s = base_ref[0, :, cut], base_ref[1, :, cut]
            turn_c, turn_s = high_c[:, cut], high_s[:, cut]
            real = (base_c * turn_c - base_s * turn_s).astype(jnp.bfloat16)
            imag = (base_c * turn_s + base_s * turn_c).astype(jnp.bfloat16)
            both = jnp.concatenate([real, imag], axis=1)
            part = jnp.dot(block, both, preferred_element_type=jnp.float32)
            acc_ref[:fields, cut] += part[:, :128]
            acc_ref[fields:, cut] += part[:, 128:]

    wave = lax.broadcasted_iota(jnp.int32, acc_ref.shape, 1)
    coefs = jnp.where(wave < points // 2, acc_ref[...], 0.0).astype(jnp.bfloat16)
    padded = mine_ref.shape[1]

    def fill(other):
        held = slots_ref[pl.ds(pl.multiple_of(other * padded, 16), padded)]
        pick = held == lax.broadcasted_iota(jnp.int32, (padded, waves), 1)
        pick = jnp.where(pick, 1.0, 0.0).astype(jnp.bfloat16)
        mine_ref[other] = lax.dot_general(
            pick, coefs, (((1,), (1,)), ((), ())), preferred_element_type=jnp.float32
        ).astype(jnp.bfloat16)

    @pl.loop(1, lat_count)
    def _(step):
        fill((lat + step) % lat_count)
        lat_copy(step).start()

    fill(lat)
    own_coefs = pltpu.make_async_copy(mine_ref.at[lat], coef_out.at[group, lat], local_sem.at[1])
    own_coefs.start()
    own_coefs.wait()

    @pl.loop(1, lat_count)
    def _(step):
        lat_copy(step).wait_recv()

    @pl.loop(1, groups)
    def _(step):
        group_copy(step).start()

    for copy in halo_copies():
        copy.wait()
    own_weights.wait()

    @pl.loop(1, groups)
    def _(step):
        weight_copy(step).wait()

    @pl.loop(1, lat_count)
    def _(step):
        lat_copy(step).wait_send()

    @pl.loop(1, groups)
    def _(step):
        group_copy(step).wait()


def exchange(sizes, points, table, slots, state, weights, halo):
    fields, width = state.shape
    waves = table.shape[2]
    sec_count, lat_count, col_count = sizes
    groups = sec_count * col_count
    padded = weights.shape[2]
    anywhere = pl.BlockSpec(memory_space=pl.ANY)
    inside = pl.BlockSpec(memory_space=pltpu.VMEM)
    halo_shapes = [jax.ShapeDtypeStruct(part.shape, part.dtype) for part in halo]
    out = pl.pallas_call(
        functools.partial(exchange_kernel, sizes),
        out_shape=[
            jax.ShapeDtypeStruct((groups, lat_count, padded, 2 * fields), jnp.bfloat16),
            jax.ShapeDtypeStruct(weights.shape, jnp.bfloat16),
        ]
        + halo_shapes
        + halo_shapes,
        in_specs=[pl.BlockSpec(memory_space=pltpu.SMEM), inside, inside, inside, anywhere]
        + [anywhere] * 5,
        out_specs=[anywhere] * 12,
        scratch_shapes=[
            pltpu.VMEM((2, CHUNK, waves), jnp.float32),
            pltpu.VMEM((2 * fields, waves), jnp.float32),
            pltpu.VMEM((lat_count, padded, 2 * fields), jnp.bfloat16),
            pltpu.SemaphoreType.DMA((2,)),
            pltpu.SemaphoreType.DMA((groups,)),
            pltpu.SemaphoreType.DMA((groups,)),
            pltpu.SemaphoreType.DMA((2, 5)),
            pltpu.SemaphoreType.DMA((2, 5)),
            pltpu.SemaphoreType.DMA((lat_count,)),
            pltpu.SemaphoreType.DMA((lat_count,)),
            pltpu.SemaphoreType.DMA((groups,)),
            pltpu.SemaphoreType.DMA((groups,)),
        ],
        compiler_params=pltpu.CompilerParams(
            vmem_limit_bytes=24 * 2**20, collective_id=0, has_side_effects=True
        ),
        cost_estimate=pl.CostEstimate(
            flops=4 * fields * waves * width, bytes_accessed=8 * 2**20, transcendentals=0
        ),
    )(points, table, slots, state, weights, *halo)
    return out[0], out[1], out[2:7], out[7:12]


def legendre_kernel(degree_ref, slots_ref, weight_ref, coef_ref, out_ref):
    rows, pair, width = coef_ref.shape
    degrees = out_ref.shape[1]
    first = degree_ref[0]
    for half in range(pair // 8):
        cut = slice(half * 8, half * 8 + 8)
        values = weight_ref[:, cut, :].astype(jnp.float32).reshape(rows * 8, weight_ref.shape[2])
        values = values.T[:degrees]
        lane_slot = lax.broadcasted_iota(jnp.int32, (degrees, rows * 8), 1) % 8
        coefs = coef_ref[:, cut, :].astype(jnp.float32).reshape(rows * 8, width).astype(jnp.bfloat16)
        degree = first + lax.broadcasted_iota(jnp.int32, (degrees, width), 0)
        for s in range(8):
            wave = slots_ref[pl.program_id(0) * pair + half * 8 + s]
            left = jnp.where(lane_slot == s, values, 0.0).astype(jnp.bfloat16)
            summed = jnp.dot(left, coefs, preferred_element_type=jnp.float32)
            out_ref[half * 8 + s] = jnp.where(degree >= wave, summed, 0.0)


def legendre(weights, coefs, slots, first_degree, slot_count, degrees):
    rows, padded, width = coefs.shape
    return pl.pallas_call(
        legendre_kernel,
        grid=(padded // SLOT_PAD,),
        out_shape=jax.ShapeDtypeStruct((slot_count, degrees, width), jnp.float32),
        in_specs=[
            pl.BlockSpec(memory_space=pltpu.SMEM),
            pl.BlockSpec(memory_space=pltpu.SMEM),
            pl.BlockSpec((rows, SLOT_PAD, weights.shape[2]), lambda i: (0, i, 0)),
            pl.BlockSpec((rows, SLOT_PAD, width), lambda i: (0, i, 0)),
        ],
        out_specs=pl.BlockSpec((SLOT_PAD, degrees, width), lambda i: (i, 0, 0)),
        compiler_params=pltpu.CompilerParams(vmem_limit_bytes=40 * 2**20),
        cost_estimate=pl.CostEstimate(
            flops=2 * rows * padded * width * degrees * 8,
            bytes_accessed=4 * slot_count * degrees * width + 4 * rows * padded * width,
            transcendentals=0,
        ),
    )(first_degree, slots, weights, coefs)


def split_two(values):
    top = lax.reduce_precision(values, 8, 7)
    return [top.astype(jnp.bfloat16), (values - top).astype(jnp.bfloat16)]


def pick_points(arrays, index):
    length = arrays[0].shape[0]
    tiles = -(-length // 128)
    matrix = jnp.stack(arrays).reshape(len(arrays), tiles, 128)
    chosen = (jnp.arange(tiles, dtype=jnp.int32)[:, None] == index[None, :] // 128).astype(jnp.bfloat16)
    spread = jnp.einsum("kta,tx->kax", matrix, chosen, preferred_element_type=jnp.float32)
    lane = jnp.arange(128, dtype=jnp.int32)[:, None] == index[None, :] % 128
    return jnp.where(lane[None], spread, 0.0).sum(axis=1)


def shifted(array, axis, count, step):
    pairs = [(i, i + step) for i in range(count) if 0 <= i + step < count]
    return lax.ppermute(array, axis, pairs)


def advance_coupled_model(
    bordered_array,
    meridian_exchange_factor,
    zonal_exchange_factor,
    depthwise_exchange_factor,
    boundary_warming_term,
):
    centre = bordered_array[:, 1:-1]
    meridional = meridian_exchange_factor[1:] * (
        bordered_array[:, 2:] - centre
    ) - meridian_exchange_factor[:-1] * (centre - bordered_array[:, :-2])
    east_flux = zonal_exchange_factor * (jnp.roll(centre, -1, axis=2) - centre)
    zonal_div = east_flux - jnp.roll(east_flux, 1, axis=2)
    vertical_flux = depthwise_exchange_factor * (centre[1:] - centre[:-1])
    zero_layer = jnp.zeros_like(vertical_flux[:1])
    vertical = jnp.concatenate([vertical_flux, zero_layer], 0) - jnp.concatenate(
        [zero_layer, vertical_flux], 0
    )
    forced = jnp.concatenate([boundary_warming_term[None], jnp.zeros_like(centre[1:])], 0)
    return centre + meridional + zonal_div + vertical + forced


def body(
    physical_state,
    parallel_lengths,
    zonal_mode_assignment,
    weighted_associated_polynomials,
    marine_tracer_state,
    lateral_diffusivity,
    depthwise_diffusivity,
    water_indicator,
    overlying_parallel,
    underlying_marine_parallel,
):
    lat_count = lax.axis_size("lat")
    groups = lax.axis_size("sec") * lax.axis_size("col")
    devices = groups * lat_count
    grid_width = physical_state.shape[2]
    strata = physical_state.shape[1] // 4
    slot_count, wave_count, row_count = weighted_associated_polynomials.shape
    block_degrees = wave_count // groups
    padded = -(-slot_count // SLOT_PAD) * SLOT_PAD
    linear_index = (
        lax.axis_index("sec") * lat_count + lax.axis_index("lat")
    ) * lax.axis_size("col") + lax.axis_index("col")
    group_index = lax.axis_index("sec") * lax.axis_size("col") + lax.axis_index("col")
    points = parallel_lengths[0]

    rows = marine_tracer_state.shape[1]
    span = marine_tracer_state.shape[2]
    layers = marine_tracer_state.shape[0]
    relative = overlying_parallel - linear_index
    halo = [
        marine_tracer_state,
        lateral_diffusivity,
        depthwise_diffusivity,
        water_indicator,
        jnp.broadcast_to(jnp.tile(relative, 2)[:, None], (2 * rows, 128)),
    ]

    send = weighted_associated_polynomials.reshape(slot_count, groups, block_degrees, row_count)
    send = jnp.transpose(send, (1, 3, 0, 2))
    send = jnp.pad(send, ((0, 0), (0, 0), (0, padded - slot_count), (0, 128 - block_degrees)))
    slots = zonal_mode_assignment.reshape(lat_count, slot_count)
    slots = jnp.pad(slots, ((0, 0), (0, padded - slot_count)), constant_values=wave_count)
    coefs, weights, before, after = exchange(
        (lax.axis_size("sec"), lat_count, lax.axis_size("col")),
        parallel_lengths,
        angle_tables(points, wave_count, grid_width),
        slots.reshape(-1, 1),
        physical_state[0],
        send,
        halo,
    )
    coefs = coefs.reshape(groups * lat_count, padded, coefs.shape[3])
    weights = weights.reshape(groups * row_count, padded, 128)
    first, last = linear_index == 0, linear_index == devices - 1
    before = [jnp.where(first, jnp.zeros_like(part), part) for part in before]
    after = [jnp.where(last, jnp.zeros_like(part), part) for part in after]

    surface = jnp.concatenate([before[0][0], marine_tracer_state[0], after[0][0]], axis=0)
    under = underlying_marine_parallel[0] - (linear_index - 1) * rows
    skin = jnp.where(jnp.arange(3 * rows)[:, None] == under, surface, 0.0).sum(axis=0)
    ocean_points = jnp.arange(span, dtype=jnp.int32)
    column = ocean_points * points // span
    sea_column = jnp.minimum(column * span // points, span - 1)
    skin_hi, skin_lo = split_two(skin)
    mapped = pick_points([skin_hi, skin_lo], sea_column)
    bottom = strata - 1
    zonal_wind = physical_state[0, bottom].astype(jnp.float32)
    meridional_wind = physical_state[0, strata + bottom].astype(jnp.float32)
    speed = thermal_transfer_factor * jnp.sqrt(
        zonal_wind * zonal_wind + meridional_wind * meridional_wind + 1.0
    )
    speed_hi, speed_lo = split_two(speed)
    picked = pick_points([speed_hi, speed_lo, physical_state[0, 2 * strata + bottom]], column)
    flux = (picked[0] + picked[1]) * (mapped[0] + mapped[1] - picked[2])
    flux_near = {
        step: shifted(flux, LINE, devices, -step) if step else flux for step in (-2, -1, 0, 1, 2)
    }

    thermal = jnp.concatenate([before[0], marine_tracer_state, after[0]], axis=1)
    kappa, depth, sea = (
        jnp.concatenate([before[k], halo[k], after[k]], axis=0) for k in (1, 2, 3)
    )
    sea = sea.astype(jnp.float32)
    relative = jnp.concatenate([before[4][:rows, :1], relative[:, None], after[4][:rows, :1]], axis=0)
    owner = jnp.arange(3 * rows, dtype=jnp.int32)[:, None] // rows - 1
    target = relative + owner
    forcing = jnp.zeros_like(sea)
    for step, row in flux_near.items():
        forcing = jnp.where(target == step, row[None], forcing)
    source = force_coef * sea * forcing
    depthwise = depth * sea
    faces = 0.5 * (kappa[:-1] + kappa[1:]) * sea[:-1] * sea[1:]
    east = 0.5 * (kappa + jnp.roll(kappa, -1, axis=1)) * sea * jnp.roll(sea, -1, axis=1)
    total = 3 * rows
    for iteration in range(OSTEPS):
        a, b = iteration + 1, total - iteration - 1
        thermal = advance_coupled_model(
            thermal, faces[a - 1 : b], east[a:b], depthwise[a:b], source[a:b]
        )

    own_waves = lax.dynamic_slice_in_dim(
        slots.reshape(-1), lax.axis_index("lat") * padded, padded
    )
    first_degree = jnp.reshape(group_index * block_degrees, (1,)).astype(jnp.int32)
    harmonic = legendre(weights, coefs, own_waves, first_degree, slot_count, block_degrees)
    return (jnp.transpose(harmonic, (1, 0, 2)), thermal)


def solution(mesh):
    return jax.shard_map(
        body,
        mesh=mesh,
        in_specs=(
            P(LINE, None, None),
            P(LINE),
            P(),
            P("lat", None, GROUP),
            P(None, LINE, None),
            P(LINE, None),
            P(LINE, None),
            P(LINE, None),
            P(LINE),
            P(LINE),
        ),
        out_specs=(P(GROUP, "lat", None), P(None, LINE, None)),
        check_vma=False,
    )
```

```python
import functools

import jax
import jax.numpy as jnp
from jax import lax
from jax.experimental import pallas as pl
from jax.experimental.pallas import tpu as pltpu
from jax.sharding import PartitionSpec as P

OSTEPS = 4
LOW = 8
CHUNK = 256
SLOT_PAD = 16

two_pi = 6.283185307179586
thermal_transfer_factor = 0.8
force_coef = 0.1

GROUP = ("sec", "col")
LINE = ("sec", "lat", "col")


def angle_tables(points, wave_count, grid_width):
    low = jnp.arange(LOW, dtype=jnp.float32)
    mid = jnp.arange(CHUNK // LOW, dtype=jnp.float32) * LOW
    high = jnp.arange(grid_width // CHUNK, dtype=jnp.float32) * CHUNK
    place = jnp.concatenate([low, mid, high])
    count = points.astype(jnp.float32)
    product = place[:, None] * jnp.arange(wave_count, dtype=jnp.float32)[None, :]
    residue = product - jnp.round(product / count) * count
    angle = residue * (jnp.float32(two_pi) / count)
    scale = jnp.where(jnp.arange(place.shape[0]) >= LOW + CHUNK // LOW, 1.0 / jnp.sqrt(count), 1.0)
    return jnp.stack([jnp.cos(angle), -jnp.sin(angle)]) * scale[None, :, None]


MESH = pl.DeviceIdType.MESH


def place_of(index, lat_count, col_count):
    return {
        "sec": index // (lat_count * col_count),
        "lat": index // col_count % lat_count,
        "col": index % col_count,
    }


def exchange_kernel(
    sizes,
    points_ref,
    table_ref,
    slots_ref,
    x_ref,
    weight_ref,
    *refs,
):
    sec_count, lat_count, col_count = sizes
    halo, coef_out, weight_out, before, after = refs[:5]
    (base_ref, acc_ref, mine_ref, local_sem, weight_send, weight_recv, halo_send, halo_recv,
     lat_send, lat_recv, sec_send, sec_recv, col_send, col_recv) = refs[5:]
    groups = sec_count * col_count
    devices = groups * lat_count
    sec, lat, col = (lax.axis_index(name) for name in LINE)
    group = sec * col_count + col
    line = (sec * lat_count + lat) * col_count + col
    following = place_of((line + 1) % devices, lat_count, col_count)
    previous = place_of((line + devices - 1) % devices, lat_count, col_count)

    def group_place(step):
        other = (group + step) % groups
        return other, {"sec": other // col_count, "lat": lat, "col": other % col_count}

    def lat_place(step):
        other = (lat + step) % lat_count
        return other, {"sec": sec, "lat": other, "col": col}

    barrier = pltpu.get_barrier_semaphore()
    for place in (following, previous):
        pl.semaphore_signal(barrier, inc=1, device_id=place, device_id_type=MESH)

    @pl.loop(1, groups)
    def _(step):
        pl.semaphore_signal(barrier, inc=1, device_id=group_place(step)[1], device_id_type=MESH)

    @pl.loop(1, lat_count)
    def _(step):
        pl.semaphore_signal(barrier, inc=1, device_id=lat_place(step)[1], device_id_type=MESH)

    pl.semaphore_wait(barrier, groups + lat_count)

    def weight_copy(step):
        other, place = group_place(step)
        return pltpu.make_async_remote_copy(
            src_ref=weight_ref.at[other],
            dst_ref=weight_out.at[group],
            send_sem=weight_send.at[step],
            recv_sem=weight_recv.at[step],
            device_id=place,
            device_id_type=MESH,
        )

    def halo_copy(side):
        return pltpu.make_async_remote_copy(
            src_ref=halo,
            dst_ref=(before, after)[side],
            send_sem=halo_send.at[side],
            recv_sem=halo_recv.at[side],
            device_id=(following, previous)[side],
            device_id_type=MESH,
        )

    has_next, has_previous = line < devices - 1, line > 0

    def lat_copy(step):
        other, place = lat_place(step)
        return pltpu.make_async_remote_copy(
            src_ref=mine_ref.at[other],
            dst_ref=coef_out.at[group, lat],
            send_sem=lat_send.at[step],
            recv_sem=lat_recv.at[step],
            device_id=place,
            device_id_type=MESH,
        )

    def sec_copy(step):
        return pltpu.make_async_remote_copy(
            src_ref=coef_out.at[group],
            dst_ref=coef_out.at[group],
            send_sem=sec_send.at[step],
            recv_sem=sec_recv.at[step],
            device_id={"sec": (sec + step) % sec_count, "lat": lat, "col": col},
            device_id_type=MESH,
        )

    def col_copy(back, step):
        block = (sec + sec_count - back) % sec_count * col_count + col
        return pltpu.make_async_remote_copy(
            src_ref=coef_out.at[block],
            dst_ref=coef_out.at[block],
            send_sem=col_send.at[back, step],
            recv_sem=col_recv.at[back, step],
            device_id={"sec": sec, "lat": lat, "col": (col + step) % col_count},
            device_id_type=MESH,
        )

    own_weights = pltpu.make_async_copy(weight_ref.at[group], weight_out.at[group], local_sem.at[0])
    own_weights.start()

    @pl.loop(1, groups)
    def _(step):
        weight_copy(step).start()

    @pl.when(has_next)
    def _():
        halo_copy(0).start()

    @pl.when(has_previous)
    def _():
        halo_copy(1).start()

    points = points_ref[0]
    waves = table_ref.shape[2]
    fields = x_ref.shape[0]
    chunks = x_ref.shape[1] // CHUNK
    low_c, low_s = table_ref[0, :LOW], table_ref[1, :LOW]
    for b in range(CHUNK // LOW):
        mid_c = table_ref[0, LOW + b : LOW + b + 1]
        mid_s = table_ref[1, LOW + b : LOW + b + 1]
        base_ref[0, b * LOW : (b + 1) * LOW] = low_c * mid_c - low_s * mid_s
        base_ref[1, b * LOW : (b + 1) * LOW] = low_c * mid_s + low_s * mid_c
    acc_ref[...] = jnp.zeros_like(acc_ref)
    top = LOW + CHUNK // LOW

    @pl.loop(0, chunks)
    def _(a):
        start = pl.multiple_of(a * CHUNK, CHUNK)
        position = start + lax.broadcasted_iota(jnp.int32, (fields, CHUNK), 1)
        block = x_ref[:, pl.ds(start, CHUNK)].astype(jnp.float32)
        block = jnp.where(position < points, block, 0.0).astype(jnp.bfloat16)
        high_c = table_ref[0, pl.ds(top + a, 1)]
        high_s = table_ref[1, pl.ds(top + a, 1)]
        for w in range(0, waves, 128):
            cut = slice(w, w + 128)
            base_c, base_s = base_ref[0, :, cut], base_ref[1, :, cut]
            turn_c, turn_s = high_c[:, cut], high_s[:, cut]
            real = (base_c * turn_c - base_s * turn_s).astype(jnp.bfloat16)
            imag = (base_c * turn_s + base_s * turn_c).astype(jnp.bfloat16)
            both = jnp.concatenate([real, imag], axis=1)
            part = jnp.dot(block, both, preferred_element_type=jnp.float32)
            acc_ref[:fields, cut] += part[:, :128]
            acc_ref[fields:, cut] += part[:, 128:]

    wave = lax.broadcasted_iota(jnp.int32, acc_ref.shape, 1)
    coefs = jnp.where(wave < points // 2, acc_ref[...], 0.0).astype(jnp.bfloat16)
    padded = mine_ref.shape[1]

    def fill(other):
        held = slots_ref[pl.ds(pl.multiple_of(other * padded, 16), padded)]
        pick = held == lax.broadcasted_iota(jnp.int32, (padded, waves), 1)
        pick = jnp.where(pick, 1.0, 0.0).astype(jnp.bfloat16)
        mine_ref[other] = lax.dot_general(
            pick, coefs, (((1,), (1,)), ((), ())), preferred_element_type=jnp.float32
        ).astype(jnp.bfloat16)

    @pl.loop(1, lat_count)
    def _(step):
        fill((lat + step) % lat_count)
        lat_copy(step).start()

    fill(lat)
    own_coefs = pltpu.make_async_copy(mine_ref.at[lat], coef_out.at[group, lat], local_sem.at[1])
    own_coefs.start()
    own_coefs.wait()

    @pl.loop(1, lat_count)
    def _(step):
        lat_copy(step).wait_recv()

    @pl.loop(1, sec_count)
    def _(step):
        sec_copy(step).start()

    @pl.loop(1, col_count)
    def _(step):
        col_copy(0, step).start()

    @pl.loop(1, sec_count)
    def _(back):
        sec_copy(back).wait_recv()

        @pl.loop(1, col_count)
        def _(step):
            col_copy(back, step).start()

    @pl.when(has_next)
    def _():
        halo_copy(0).wait_send()
        halo_copy(1).wait_recv()

    @pl.when(has_previous)
    def _():
        halo_copy(1).wait_send()
        halo_copy(0).wait_recv()

    own_weights.wait()

    @pl.loop(1, groups)
    def _(step):
        weight_copy(step).wait()

    @pl.loop(1, lat_count)
    def _(step):
        lat_copy(step).wait_send()

    @pl.loop(1, sec_count)
    def _(step):
        sec_copy(step).wait_send()

    @pl.loop(0, sec_count)
    def _(back):
        @pl.loop(1, col_count)
        def _(step):
            col_copy(back, step).wait()


def exchange(sizes, points, table, slots, state, weights, halo):
    fields, width = state.shape
    waves = table.shape[2]
    sec_count, lat_count, col_count = sizes
    groups = sec_count * col_count
    padded = weights.shape[1]
    anywhere = pl.BlockSpec(memory_space=pl.ANY)
    inside = pl.BlockSpec(memory_space=pltpu.VMEM)
    halo_shape = jax.ShapeDtypeStruct(halo.shape, halo.dtype)
    out = pl.pallas_call(
        functools.partial(exchange_kernel, sizes),
        out_shape=[
            jax.ShapeDtypeStruct((groups, lat_count, padded, 2 * fields), jnp.bfloat16),
            jax.ShapeDtypeStruct(weights.shape, jnp.bfloat16),
            halo_shape,
            halo_shape,
        ],
        in_specs=[pl.BlockSpec(memory_space=pltpu.SMEM), inside, inside, inside, anywhere, anywhere],
        out_specs=[anywhere] * 4,
        scratch_shapes=[
            pltpu.VMEM((2, CHUNK, waves), jnp.float32),
            pltpu.VMEM((2 * fields, waves), jnp.float32),
            pltpu.VMEM((lat_count, padded, 2 * fields), jnp.bfloat16),
            pltpu.SemaphoreType.DMA((2,)),
            pltpu.SemaphoreType.DMA((groups,)),
            pltpu.SemaphoreType.DMA((groups,)),
            pltpu.SemaphoreType.DMA((2,)),
            pltpu.SemaphoreType.DMA((2,)),
            pltpu.SemaphoreType.DMA((lat_count,)),
            pltpu.SemaphoreType.DMA((lat_count,)),
            pltpu.SemaphoreType.DMA((sec_count,)),
            pltpu.SemaphoreType.DMA((sec_count,)),
            pltpu.SemaphoreType.DMA((sec_count, col_count)),
            pltpu.SemaphoreType.DMA((sec_count, col_count)),
        ],
        compiler_params=pltpu.CompilerParams(
            vmem_limit_bytes=24 * 2**20, collective_id=0, has_side_effects=True
        ),
        cost_estimate=pl.CostEstimate(
            flops=4 * fields * waves * width, bytes_accessed=8 * 2**20, transcendentals=0
        ),
    )(points, table, slots, state, weights, halo)
    return out


def legendre_kernel(degree_ref, slots_ref, weight_ref, coef_ref, out_ref):
    groups, lines, pair, width = coef_ref.shape
    rows = groups * lines
    packed = weight_ref.shape[2]
    degrees = out_ref.shape[1]
    first = degree_ref[0]
    for half in range(pair // 8):
        cut = slice(half * 8, half * 8 + 8)
        held = weight_ref[:, cut, :].astype(jnp.float32).reshape(groups * 8, packed)
        parts = [
            pltpu.roll(held, (packed - q * degrees) % packed, 1)[:, :128] if q else held[:, :128]
            for q in range(lines)
        ]
        values = jnp.concatenate(parts, axis=0).T[:degrees]
        lane_slot = lax.broadcasted_iota(jnp.int32, (degrees, rows * 8), 1) % 8
        coefs = jnp.concatenate(
            [
                coef_ref[:, q, cut, :].astype(jnp.float32).reshape(groups * 8, width)
                for q in range(lines)
            ],
            axis=0,
        ).astype(jnp.bfloat16)
        degree = first + lax.broadcasted_iota(jnp.int32, (degrees, width), 0)
        for s in range(8):
            wave = slots_ref[pl.program_id(0) * pair + half * 8 + s]
            left = jnp.where(lane_slot == s, values, 0.0).astype(jnp.bfloat16)
            summed = jnp.dot(left, coefs, preferred_element_type=jnp.float32)
            out_ref[half * 8 + s] = jnp.where(degree >= wave, summed, 0.0)


def legendre(weights, coefs, slots, first_degree, slot_count, degrees):
    groups, lines, padded, width = coefs.shape
    rows = groups * lines
    return pl.pallas_call(
        legendre_kernel,
        grid=(padded // SLOT_PAD,),
        out_shape=jax.ShapeDtypeStruct((slot_count, degrees, width), jnp.float32),
        in_specs=[
            pl.BlockSpec(memory_space=pltpu.SMEM),
            pl.BlockSpec(memory_space=pltpu.SMEM),
            pl.BlockSpec((groups, SLOT_PAD, weights.shape[2]), lambda i: (0, i, 0)),
            pl.BlockSpec((groups, lines, SLOT_PAD, width), lambda i: (0, 0, i, 0)),
        ],
        out_specs=pl.BlockSpec((SLOT_PAD, degrees, width), lambda i: (i, 0, 0)),
        compiler_params=pltpu.CompilerParams(vmem_limit_bytes=(8 if rows <= 64 else 32) * 2**20),
        cost_estimate=pl.CostEstimate(
            flops=2 * rows * padded * width * degrees * 8,
            bytes_accessed=4 * slot_count * degrees * width + 4 * rows * padded * width,
            transcendentals=0,
        ),
    )(first_degree, slots, weights, coefs)


def split_two(values):
    top = lax.reduce_precision(values, 8, 7)
    return [top.astype(jnp.bfloat16), (values - top).astype(jnp.bfloat16)]


def pick_points(arrays, index):
    length = arrays[0].shape[0]
    tiles = -(-length // 128)
    matrix = jnp.stack(arrays).reshape(len(arrays), tiles, 128)
    chosen = (jnp.arange(tiles, dtype=jnp.int32)[:, None] == index[None, :] // 128).astype(jnp.bfloat16)
    spread = jnp.einsum("kta,tx->kax", matrix, chosen, preferred_element_type=jnp.float32)
    lane = jnp.arange(128, dtype=jnp.int32)[:, None] == index[None, :] % 128
    return jnp.where(lane[None], spread, 0.0).sum(axis=1)


def shifted(array, axis, count, step):
    pairs = [(i, i + step) for i in range(count) if 0 <= i + step < count]
    return lax.ppermute(array, axis, pairs)


def advance_coupled_model(
    bordered_array,
    meridian_exchange_factor,
    zonal_exchange_factor,
    depthwise_exchange_factor,
    boundary_warming_term,
):
    centre = bordered_array[:, 1:-1]
    meridional = meridian_exchange_factor[1:] * (
        bordered_array[:, 2:] - centre
    ) - meridian_exchange_factor[:-1] * (centre - bordered_array[:, :-2])
    east_flux = zonal_exchange_factor * (jnp.roll(centre, -1, axis=2) - centre)
    zonal_div = east_flux - jnp.roll(east_flux, 1, axis=2)
    vertical_flux = depthwise_exchange_factor * (centre[1:] - centre[:-1])
    zero_layer = jnp.zeros_like(vertical_flux[:1])
    vertical = jnp.concatenate([vertical_flux, zero_layer], 0) - jnp.concatenate(
        [zero_layer, vertical_flux], 0
    )
    forced = jnp.concatenate([boundary_warming_term[None], jnp.zeros_like(centre[1:])], 0)
    return centre + meridional + zonal_div + vertical + forced


def body(
    physical_state,
    parallel_lengths,
    zonal_mode_assignment,
    weighted_associated_polynomials,
    marine_tracer_state,
    lateral_diffusivity,
    depthwise_diffusivity,
    water_indicator,
    overlying_parallel,
    underlying_marine_parallel,
):
    lat_count = lax.axis_size("lat")
    groups = lax.axis_size("sec") * lax.axis_size("col")
    devices = groups * lat_count
    grid_width = physical_state.shape[2]
    strata = physical_state.shape[1] // 4
    slot_count, wave_count, row_count = weighted_associated_polynomials.shape
    block_degrees = wave_count // groups
    padded = -(-slot_count // SLOT_PAD) * SLOT_PAD
    linear_index = (
        lax.axis_index("sec") * lat_count + lax.axis_index("lat")
    ) * lax.axis_size("col") + lax.axis_index("col")
    group_index = lax.axis_index("sec") * lax.axis_size("col") + lax.axis_index("col")
    points = parallel_lengths[0]

    rows = marine_tracer_state.shape[1]
    span = marine_tracer_state.shape[2]
    layers = marine_tracer_state.shape[0]
    relative = overlying_parallel - linear_index
    payload = jnp.concatenate(
        [
            marine_tracer_state,
            lateral_diffusivity[None],
            depthwise_diffusivity[None],
            water_indicator.astype(jnp.float32)[None],
            jnp.broadcast_to(relative.astype(jnp.float32)[:, None], (rows, span))[None],
        ],
        axis=0,
    )
    halo = payload.astype(jnp.bfloat16).reshape((layers + 4) * rows, span)

    send = weighted_associated_polynomials.reshape(slot_count, groups, block_degrees, row_count)
    send = jnp.transpose(send, (1, 0, 3, 2)).reshape(groups, slot_count, row_count * block_degrees)
    lanes = -(-send.shape[2] // 128) * 128
    send = jnp.pad(send, ((0, 0), (0, padded - slot_count), (0, lanes - send.shape[2])))
    slots = zonal_mode_assignment.reshape(lat_count, slot_count)
    slots = jnp.pad(slots, ((0, 0), (0, padded - slot_count)), constant_values=wave_count)
    coefs, weights, before, after = exchange(
        (lax.axis_size("sec"), lat_count, lax.axis_size("col")),
        parallel_lengths,
        angle_tables(points, wave_count, grid_width),
        slots.reshape(-1, 1),
        physical_state[0],
        send,
        halo,
    )
    first, last = linear_index == 0, linear_index == devices - 1
    before = jnp.where(first, jnp.zeros_like(before), before).astype(jnp.float32)
    after = jnp.where(last, jnp.zeros_like(after), after).astype(jnp.float32)
    before = before.reshape(payload.shape)
    after = after.reshape(payload.shape)

    surface = jnp.concatenate([before[0], marine_tracer_state[0], after[0]], axis=0)
    under = underlying_marine_parallel[0] - (linear_index - 1) * rows
    skin = jnp.where(jnp.arange(3 * rows)[:, None] == under, surface, 0.0).sum(axis=0)
    ocean_points = jnp.arange(span, dtype=jnp.int32)
    column = ocean_points * points // span
    sea_column = jnp.minimum(column * span // points, span - 1)
    skin_hi, skin_lo = split_two(skin)
    mapped = pick_points([skin_hi, skin_lo], sea_column)
    bottom = strata - 1
    zonal_wind = physical_state[0, bottom].astype(jnp.float32)
    meridional_wind = physical_state[0, strata + bottom].astype(jnp.float32)
    speed = thermal_transfer_factor * jnp.sqrt(
        zonal_wind * zonal_wind + meridional_wind * meridional_wind + 1.0
    )
    speed_hi, speed_lo = split_two(speed)
    picked = pick_points([speed_hi, speed_lo, physical_state[0, 2 * strata + bottom]], column)
    flux = (picked[0] + picked[1]) * (mapped[0] + mapped[1] - picked[2])
    flux_near = {
        step: shifted(flux, LINE, devices, -step) if step else flux for step in (-2, -1, 0, 1, 2)
    }

    whole = jnp.concatenate([before, payload, after], axis=1)
    thermal = whole[:layers]
    kappa, depth, sea, relative = (whole[layers + k] for k in range(4))
    owner = jnp.arange(3 * rows, dtype=jnp.int32)[:, None] // rows - 1
    target = relative + owner.astype(jnp.float32)
    forcing = jnp.zeros_like(sea)
    for step, row in flux_near.items():
        forcing = jnp.where(target == step, row[None], forcing)
    source = force_coef * sea * forcing
    depthwise = depth * sea
    faces = 0.5 * (kappa[:-1] + kappa[1:]) * sea[:-1] * sea[1:]
    east = 0.5 * (kappa + jnp.roll(kappa, -1, axis=1)) * sea * jnp.roll(sea, -1, axis=1)
    total = 3 * rows
    for iteration in range(OSTEPS):
        a, b = iteration + 1, total - iteration - 1
        thermal = advance_coupled_model(
            thermal, faces[a - 1 : b], east[a:b], depthwise[a:b], source[a:b]
        )

    own_waves = lax.dynamic_slice_in_dim(
        slots.reshape(-1), lax.axis_index("lat") * padded, padded
    )
    first_degree = jnp.reshape(group_index * block_degrees, (1,)).astype(jnp.int32)
    harmonic = legendre(weights, coefs, own_waves, first_degree, slot_count, block_degrees)
    return (jnp.transpose(harmonic, (1, 0, 2)), thermal)


def solution(mesh):
    return jax.shard_map(
        body,
        mesh=mesh,
        in_specs=(
            P(LINE, None, None),
            P(LINE),
            P(),
            P("lat", None, GROUP),
            P(None, LINE, None),
            P(LINE, None),
            P(LINE, None),
            P(LINE, None),
            P(LINE),
            P(LINE),
        ),
        out_specs=(P(GROUP, "lat", None), P(None, LINE, None)),
        check_vma=False,
    )
```

```python
import functools

import jax
import jax.numpy as jnp
from jax import lax
from jax.experimental import pallas as pl
from jax.experimental.pallas import tpu as pltpu
from jax.sharding import PartitionSpec as P

OSTEPS = 4
LOW = 8
CHUNK = 256
SLOT_PAD = 16

two_pi = 6.283185307179586
thermal_transfer_factor = 0.8
force_coef = 0.1

GROUP = ("sec", "col")
LINE = ("sec", "lat", "col")


def angle_tables(points, wave_count, grid_width):
    low = jnp.arange(LOW, dtype=jnp.float32)
    mid = jnp.arange(CHUNK // LOW, dtype=jnp.float32) * LOW
    high = jnp.arange(grid_width // CHUNK, dtype=jnp.float32) * CHUNK
    place = jnp.concatenate([low, mid, high])
    count = points.astype(jnp.float32)
    product = place[:, None] * jnp.arange(wave_count, dtype=jnp.float32)[None, :]
    residue = product - jnp.round(product / count) * count
    angle = residue * (jnp.float32(two_pi) / count)
    scale = jnp.where(jnp.arange(place.shape[0]) >= LOW + CHUNK // LOW, 1.0 / jnp.sqrt(count), 1.0)
    return jnp.stack([jnp.cos(angle), -jnp.sin(angle)]) * scale[None, :, None]


MESH = pl.DeviceIdType.MESH


def place_of(index, lat_count, col_count):
    return {
        "sec": index // (lat_count * col_count),
        "lat": index // col_count % lat_count,
        "col": index % col_count,
    }


def exchange_kernel(
    sizes,
    points_ref,
    table_ref,
    slots_ref,
    x_ref,
    weight_ref,
    *refs,
):
    sec_count, lat_count, col_count = sizes
    halo, coef_out, weight_out, before, after = refs[:5]
    (base_ref, acc_ref, mine_ref, local_sem, weight_send, weight_recv, halo_send, halo_recv,
     lat_send, lat_recv, sec_send, sec_recv, col_send, col_recv) = refs[5:]
    groups = sec_count * col_count
    devices = groups * lat_count
    sec, lat, col = (lax.axis_index(name) for name in LINE)
    group = sec * col_count + col
    line = (sec * lat_count + lat) * col_count + col
    following = place_of((line + 1) % devices, lat_count, col_count)
    previous = place_of((line + devices - 1) % devices, lat_count, col_count)

    def group_place(step):
        other = (group + step) % groups
        return other, {"sec": other // col_count, "lat": lat, "col": other % col_count}

    def lat_place(step):
        other = (lat + step) % lat_count
        return other, {"sec": sec, "lat": other, "col": col}

    barrier = pltpu.get_barrier_semaphore()
    for place in (following, previous):
        pl.semaphore_signal(barrier, inc=1, device_id=place, device_id_type=MESH)

    @pl.loop(1, groups)
    def _(step):
        pl.semaphore_signal(barrier, inc=1, device_id=group_place(step)[1], device_id_type=MESH)

    @pl.loop(1, lat_count)
    def _(step):
        pl.semaphore_signal(barrier, inc=1, device_id=lat_place(step)[1], device_id_type=MESH)

    pl.semaphore_wait(barrier, groups + lat_count)

    def weight_copy(step):
        other, place = group_place(step)
        return pltpu.make_async_remote_copy(
            src_ref=weight_ref.at[other],
            dst_ref=weight_out.at[group],
            send_sem=weight_send.at[step],
            recv_sem=weight_recv.at[step],
            device_id=place,
            device_id_type=MESH,
        )

    def halo_copy(side):
        return pltpu.make_async_remote_copy(
            src_ref=halo,
            dst_ref=(before, after)[side],
            send_sem=halo_send.at[side],
            recv_sem=halo_recv.at[side],
            device_id=(following, previous)[side],
            device_id_type=MESH,
        )

    has_next, has_previous = line < devices - 1, line > 0

    def lat_copy(step):
        other, place = lat_place(step)
        return pltpu.make_async_remote_copy(
            src_ref=mine_ref.at[other],
            dst_ref=coef_out.at[group, lat],
            send_sem=lat_send.at[step],
            recv_sem=lat_recv.at[step],
            device_id=place,
            device_id_type=MESH,
        )

    def sec_copy(step):
        return pltpu.make_async_remote_copy(
            src_ref=coef_out.at[group],
            dst_ref=coef_out.at[group],
            send_sem=sec_send.at[step],
            recv_sem=sec_recv.at[step],
            device_id={"sec": (sec + step) % sec_count, "lat": lat, "col": col},
            device_id_type=MESH,
        )

    def col_copy(back, step):
        block = (sec + sec_count - back) % sec_count * col_count + col
        return pltpu.make_async_remote_copy(
            src_ref=coef_out.at[block],
            dst_ref=coef_out.at[block],
            send_sem=col_send.at[back, step],
            recv_sem=col_recv.at[back, step],
            device_id={"sec": sec, "lat": lat, "col": (col + step) % col_count},
            device_id_type=MESH,
        )

    own_weights = pltpu.make_async_copy(weight_ref.at[group], weight_out.at[group], local_sem.at[0])
    own_weights.start()

    @pl.loop(1, groups)
    def _(step):
        weight_copy(step).start()

    @pl.when(has_next)
    def _():
        halo_copy(0).start()

    @pl.when(has_previous)
    def _():
        halo_copy(1).start()

    points = points_ref[0]
    waves = table_ref.shape[2]
    fields = x_ref.shape[0]
    chunks = x_ref.shape[1] // CHUNK
    low_c, low_s = table_ref[0, :LOW], table_ref[1, :LOW]
    for b in range(CHUNK // LOW):
        mid_c = table_ref[0, LOW + b : LOW + b + 1]
        mid_s = table_ref[1, LOW + b : LOW + b + 1]
        base_ref[0, b * LOW : (b + 1) * LOW] = low_c * mid_c - low_s * mid_s
        base_ref[1, b * LOW : (b + 1) * LOW] = low_c * mid_s + low_s * mid_c
    acc_ref[...] = jnp.zeros_like(acc_ref)
    top = LOW + CHUNK // LOW

    @pl.loop(0, chunks)
    def _(a):
        start = pl.multiple_of(a * CHUNK, CHUNK)
        position = start + lax.broadcasted_iota(jnp.int32, (fields, CHUNK), 1)
        block = x_ref[:, pl.ds(start, CHUNK)].astype(jnp.float32)
        block = jnp.where(position < points, block, 0.0).astype(jnp.bfloat16)
        high_c = table_ref[0, pl.ds(top + a, 1)]
        high_s = table_ref[1, pl.ds(top + a, 1)]
        for w in range(0, waves, 128):
            cut = slice(w, w + 128)
            base_c, base_s = base_ref[0, :, cut], base_ref[1, :, cut]
            turn_c, turn_s = high_c[:, cut], high_s[:, cut]
            real = (base_c * turn_c - base_s * turn_s).astype(jnp.bfloat16)
            imag = (base_c * turn_s + base_s * turn_c).astype(jnp.bfloat16)
            both = jnp.concatenate([real, imag], axis=1)
            part = jnp.dot(block, both, preferred_element_type=jnp.float32)
            acc_ref[:fields, cut] += part[:, :128]
            acc_ref[fields:, cut] += part[:, 128:]

    wave = lax.broadcasted_iota(jnp.int32, acc_ref.shape, 1)
    coefs = jnp.where(wave < points // 2, acc_ref[...], 0.0).astype(jnp.bfloat16)
    padded = mine_ref.shape[1]

    def fill(other):
        held = slots_ref[pl.ds(pl.multiple_of(other * padded, 16), padded)]
        pick = held == lax.broadcasted_iota(jnp.int32, (padded, waves), 1)
        pick = jnp.where(pick, 1.0, 0.0).astype(jnp.bfloat16)
        mine_ref[other] = lax.dot_general(
            pick, coefs, (((1,), (1,)), ((), ())), preferred_element_type=jnp.float32
        ).astype(jnp.bfloat16)

    @pl.loop(1, lat_count)
    def _(step):
        fill((lat + step) % lat_count)
        lat_copy(step).start()

    fill(lat)
    own_coefs = pltpu.make_async_copy(mine_ref.at[lat], coef_out.at[group, lat], local_sem.at[1])
    own_coefs.start()
    own_coefs.wait()

    @pl.loop(1, lat_count)
    def _(step):
        lat_copy(step).wait_recv()

    @pl.loop(1, sec_count)
    def _(step):
        sec_copy(step).start()

    @pl.loop(1, col_count)
    def _(step):
        col_copy(0, step).start()

    @pl.loop(1, sec_count)
    def _(back):
        sec_copy(back).wait_recv()

        @pl.loop(1, col_count)
        def _(step):
            col_copy(back, step).start()

    @pl.when(has_next)
    def _():
        halo_copy(0).wait_send()
        halo_copy(1).wait_recv()

    @pl.when(has_previous)
    def _():
        halo_copy(1).wait_send()
        halo_copy(0).wait_recv()

    own_weights.wait()

    @pl.loop(1, groups)
    def _(step):
        weight_copy(step).wait()

    @pl.loop(1, lat_count)
    def _(step):
        lat_copy(step).wait_send()

    @pl.loop(1, sec_count)
    def _(step):
        sec_copy(step).wait_send()

    @pl.loop(0, sec_count)
    def _(back):
        @pl.loop(1, col_count)
        def _(step):
            col_copy(back, step).wait()


def exchange(sizes, points, table, slots, state, weights, halo):
    fields, width = state.shape
    waves = table.shape[2]
    sec_count, lat_count, col_count = sizes
    groups = sec_count * col_count
    padded = weights.shape[1]
    anywhere = pl.BlockSpec(memory_space=pl.ANY)
    inside = pl.BlockSpec(memory_space=pltpu.VMEM)
    halo_shape = jax.ShapeDtypeStruct(halo.shape, halo.dtype)
    out = pl.pallas_call(
        functools.partial(exchange_kernel, sizes),
        out_shape=[
            jax.ShapeDtypeStruct((groups, lat_count, padded, 2 * fields), jnp.bfloat16),
            jax.ShapeDtypeStruct(weights.shape, jnp.bfloat16),
            halo_shape,
            halo_shape,
        ],
        in_specs=[pl.BlockSpec(memory_space=pltpu.SMEM), inside, inside, inside, anywhere, anywhere],
        out_specs=[anywhere] * 4,
        scratch_shapes=[
            pltpu.VMEM((2, CHUNK, waves), jnp.float32),
            pltpu.VMEM((2 * fields, waves), jnp.float32),
            pltpu.VMEM((lat_count, padded, 2 * fields), jnp.bfloat16),
            pltpu.SemaphoreType.DMA((2,)),
            pltpu.SemaphoreType.DMA((groups,)),
            pltpu.SemaphoreType.DMA((groups,)),
            pltpu.SemaphoreType.DMA((2,)),
            pltpu.SemaphoreType.DMA((2,)),
            pltpu.SemaphoreType.DMA((lat_count,)),
            pltpu.SemaphoreType.DMA((lat_count,)),
            pltpu.SemaphoreType.DMA((sec_count,)),
            pltpu.SemaphoreType.DMA((sec_count,)),
            pltpu.SemaphoreType.DMA((sec_count, col_count)),
            pltpu.SemaphoreType.DMA((sec_count, col_count)),
        ],
        compiler_params=pltpu.CompilerParams(
            vmem_limit_bytes=24 * 2**20, collective_id=0, has_side_effects=True
        ),
        cost_estimate=pl.CostEstimate(
            flops=4 * fields * waves * width, bytes_accessed=8 * 2**20, transcendentals=0
        ),
    )(points, table, slots, state, weights, halo)
    return out


REACH = (-2, -1, 1, 2)


def flux_kernel(sizes, row_ref, out_ref, send_sem, recv_sem):
    sec_count, lat_count, col_count = sizes
    devices = sec_count * lat_count * col_count
    sec, lat, col = (lax.axis_index(name) for name in LINE)
    line = (sec * lat_count + lat) * col_count + col
    places = [place_of((line + devices - step) % devices, lat_count, col_count) for step in REACH]
    barrier = pltpu.get_barrier_semaphore()
    for place in places:
        pl.semaphore_signal(barrier, inc=1, device_id=place, device_id_type=MESH)
    pl.semaphore_wait(barrier, len(REACH))
    copies = [
        pltpu.make_async_remote_copy(
            src_ref=row_ref,
            dst_ref=out_ref.at[k],
            send_sem=send_sem.at[k],
            recv_sem=recv_sem.at[k],
            device_id=place,
            device_id_type=MESH,
        )
        for k, place in enumerate(places)
    ]
    for copy in copies:
        copy.start()
    for copy in copies:
        copy.wait()


def near_rows(sizes, row):
    shape = (8, row.shape[0] // 8)
    out = pl.pallas_call(
        functools.partial(flux_kernel, sizes),
        out_shape=jax.ShapeDtypeStruct((len(REACH),) + shape, row.dtype),
        in_specs=[pl.BlockSpec(memory_space=pltpu.VMEM)],
        out_specs=pl.BlockSpec(memory_space=pltpu.VMEM),
        scratch_shapes=[pltpu.SemaphoreType.DMA((len(REACH),))] * 2,
        compiler_params=pltpu.CompilerParams(
            vmem_limit_bytes=2**20, collective_id=1, has_side_effects=True
        ),
    )(row.reshape(shape))
    return out.reshape(len(REACH), row.shape[0])


def legendre_kernel(degree_ref, slots_ref, weight_ref, coef_ref, out_ref):
    groups, lines, pair, width = coef_ref.shape
    rows = groups * lines
    packed = weight_ref.shape[2]
    degrees = out_ref.shape[1]
    first = degree_ref[0]
    for half in range(pair // 8):
        cut = slice(half * 8, half * 8 + 8)
        held = weight_ref[:, cut, :].astype(jnp.float32).reshape(groups * 8, packed)
        parts = [
            pltpu.roll(held, (packed - q * degrees) % packed, 1)[:, :128] if q else held[:, :128]
            for q in range(lines)
        ]
        values = jnp.concatenate(parts, axis=0).T[:degrees]
        lane_slot = lax.broadcasted_iota(jnp.int32, (degrees, rows * 8), 1) % 8
        coefs = jnp.concatenate(
            [
                coef_ref[:, q, cut, :].astype(jnp.float32).reshape(groups * 8, width)
                for q in range(lines)
            ],
            axis=0,
        ).astype(jnp.bfloat16)
        degree = first + lax.broadcasted_iota(jnp.int32, (degrees, width), 0)
        for s in range(8):
            wave = slots_ref[pl.program_id(0) * pair + half * 8 + s]
            left = jnp.where(lane_slot == s, values, 0.0).astype(jnp.bfloat16)
            summed = jnp.dot(left, coefs, preferred_element_type=jnp.float32)
            out_ref[half * 8 + s] = jnp.where(degree >= wave, summed, 0.0)


def legendre(weights, coefs, slots, first_degree, slot_count, degrees):
    groups, lines, padded, width = coefs.shape
    rows = groups * lines
    return pl.pallas_call(
        legendre_kernel,
        grid=(padded // SLOT_PAD,),
        out_shape=jax.ShapeDtypeStruct((slot_count, degrees, width), jnp.float32),
        in_specs=[
            pl.BlockSpec(memory_space=pltpu.SMEM),
            pl.BlockSpec(memory_space=pltpu.SMEM),
            pl.BlockSpec((groups, SLOT_PAD, weights.shape[2]), lambda i: (0, i, 0)),
            pl.BlockSpec((groups, lines, SLOT_PAD, width), lambda i: (0, 0, i, 0)),
        ],
        out_specs=pl.BlockSpec((SLOT_PAD, degrees, width), lambda i: (i, 0, 0)),
        compiler_params=pltpu.CompilerParams(vmem_limit_bytes=(8 if rows <= 64 else 32) * 2**20),
        cost_estimate=pl.CostEstimate(
            flops=2 * rows * padded * width * degrees * 8,
            bytes_accessed=4 * slot_count * degrees * width + 4 * rows * padded * width,
            transcendentals=0,
        ),
    )(first_degree, slots, weights, coefs)


def split_two(values):
    top = lax.reduce_precision(values, 8, 7)
    return [top.astype(jnp.bfloat16), (values - top).astype(jnp.bfloat16)]


def pick_points(arrays, index):
    length = arrays[0].shape[0]
    tiles = -(-length // 128)
    matrix = jnp.stack(arrays).reshape(len(arrays), tiles, 128)
    chosen = (jnp.arange(tiles, dtype=jnp.int32)[:, None] == index[None, :] // 128).astype(jnp.bfloat16)
    spread = jnp.einsum("kta,tx->kax", matrix, chosen, preferred_element_type=jnp.float32)
    lane = jnp.arange(128, dtype=jnp.int32)[:, None] == index[None, :] % 128
    return jnp.where(lane[None], spread, 0.0).sum(axis=1)


def advance_coupled_model(
    bordered_array,
    meridian_exchange_factor,
    zonal_exchange_factor,
    depthwise_exchange_factor,
    boundary_warming_term,
):
    centre = bordered_array[:, 1:-1]
    meridional = meridian_exchange_factor[1:] * (
        bordered_array[:, 2:] - centre
    ) - meridian_exchange_factor[:-1] * (centre - bordered_array[:, :-2])
    east_flux = zonal_exchange_factor * (jnp.roll(centre, -1, axis=2) - centre)
    zonal_div = east_flux - jnp.roll(east_flux, 1, axis=2)
    vertical_flux = depthwise_exchange_factor * (centre[1:] - centre[:-1])
    zero_layer = jnp.zeros_like(vertical_flux[:1])
    vertical = jnp.concatenate([vertical_flux, zero_layer], 0) - jnp.concatenate(
        [zero_layer, vertical_flux], 0
    )
    forced = jnp.concatenate([boundary_warming_term[None], jnp.zeros_like(centre[1:])], 0)
    return centre + meridional + zonal_div + vertical + forced


def body(
    physical_state,
    parallel_lengths,
    zonal_mode_assignment,
    weighted_associated_polynomials,
    marine_tracer_state,
    lateral_diffusivity,
    depthwise_diffusivity,
    water_indicator,
    overlying_parallel,
    underlying_marine_parallel,
):
    lat_count = lax.axis_size("lat")
    groups = lax.axis_size("sec") * lax.axis_size("col")
    devices = groups * lat_count
    grid_width = physical_state.shape[2]
    strata = physical_state.shape[1] // 4
    slot_count, wave_count, row_count = weighted_associated_polynomials.shape
    block_degrees = wave_count // groups
    padded = -(-slot_count // SLOT_PAD) * SLOT_PAD
    linear_index = (
        lax.axis_index("sec") * lat_count + lax.axis_index("lat")
    ) * lax.axis_size("col") + lax.axis_index("col")
    group_index = lax.axis_index("sec") * lax.axis_size("col") + lax.axis_index("col")
    points = parallel_lengths[0]

    rows = marine_tracer_state.shape[1]
    span = marine_tracer_state.shape[2]
    layers = marine_tracer_state.shape[0]
    relative = overlying_parallel - linear_index
    payload = jnp.concatenate(
        [
            marine_tracer_state,
            lateral_diffusivity[None],
            depthwise_diffusivity[None],
            water_indicator.astype(jnp.float32)[None],
            jnp.broadcast_to(relative.astype(jnp.float32)[:, None], (rows, span))[None],
        ],
        axis=0,
    )
    halo = payload.astype(jnp.bfloat16).reshape((layers + 4) * rows, span)

    send = weighted_associated_polynomials.reshape(slot_count, groups, block_degrees, row_count)
    send = jnp.transpose(send, (1, 0, 3, 2)).reshape(groups, slot_count, row_count * block_degrees)
    lanes = -(-send.shape[2] // 128) * 128
    send = jnp.pad(send, ((0, 0), (0, padded - slot_count), (0, lanes - send.shape[2])))
    slots = zonal_mode_assignment.reshape(lat_count, slot_count)
    slots = jnp.pad(slots, ((0, 0), (0, padded - slot_count)), constant_values=wave_count)
    coefs, weights, before, after = exchange(
        (lax.axis_size("sec"), lat_count, lax.axis_size("col")),
        parallel_lengths,
        angle_tables(points, wave_count, grid_width),
        slots.reshape(-1, 1),
        physical_state[0],
        send,
        halo,
    )
    first, last = linear_index == 0, linear_index == devices - 1
    before = jnp.where(first, jnp.zeros_like(before), before).astype(jnp.float32)
    after = jnp.where(last, jnp.zeros_like(after), after).astype(jnp.float32)
    before = before.reshape(payload.shape)
    after = after.reshape(payload.shape)

    surface = jnp.concatenate([before[0], marine_tracer_state[0], after[0]], axis=0)
    under = underlying_marine_parallel[0] - (linear_index - 1) * rows
    skin = jnp.where(jnp.arange(3 * rows)[:, None] == under, surface, 0.0).sum(axis=0)
    ocean_points = jnp.arange(span, dtype=jnp.int32)
    column = ocean_points * points // span
    sea_column = jnp.minimum(column * span // points, span - 1)
    skin_hi, skin_lo = split_two(skin)
    mapped = pick_points([skin_hi, skin_lo], sea_column)
    bottom = strata - 1
    zonal_wind = physical_state[0, bottom].astype(jnp.float32)
    meridional_wind = physical_state[0, strata + bottom].astype(jnp.float32)
    speed = thermal_transfer_factor * jnp.sqrt(
        zonal_wind * zonal_wind + meridional_wind * meridional_wind + 1.0
    )
    speed_hi, speed_lo = split_two(speed)
    picked = pick_points([speed_hi, speed_lo, physical_state[0, 2 * strata + bottom]], column)
    flux = (picked[0] + picked[1]) * (mapped[0] + mapped[1] - picked[2])
    near = near_rows((lax.axis_size("sec"), lat_count, lax.axis_size("col")), flux)
    flux_near = {0: flux, **{step: near[k] for k, step in enumerate(REACH)}}

    whole = jnp.concatenate([before, payload, after], axis=1)
    thermal = whole[:layers]
    kappa, depth, sea, relative = (whole[layers + k] for k in range(4))
    owner = jnp.arange(3 * rows, dtype=jnp.int32)[:, None] // rows - 1
    target = relative + owner.astype(jnp.float32)
    forcing = jnp.zeros_like(sea)
    for step, row in flux_near.items():
        forcing = jnp.where(target == step, row[None], forcing)
    source = force_coef * sea * forcing
    depthwise = depth * sea
    faces = 0.5 * (kappa[:-1] + kappa[1:]) * sea[:-1] * sea[1:]
    east = 0.5 * (kappa + jnp.roll(kappa, -1, axis=1)) * sea * jnp.roll(sea, -1, axis=1)
    total = 3 * rows
    for iteration in range(OSTEPS):
        a, b = iteration + 1, total - iteration - 1
        thermal = advance_coupled_model(
            thermal, faces[a - 1 : b], east[a:b], depthwise[a:b], source[a:b]
        )

    own_waves = lax.dynamic_slice_in_dim(
        slots.reshape(-1), lax.axis_index("lat") * padded, padded
    )
    first_degree = jnp.reshape(group_index * block_degrees, (1,)).astype(jnp.int32)
    harmonic = legendre(weights, coefs, own_waves, first_degree, slot_count, block_degrees)
    return (jnp.transpose(harmonic, (1, 0, 2)), thermal)


def solution(mesh):
    return jax.shard_map(
        body,
        mesh=mesh,
        in_specs=(
            P(LINE, None, None),
            P(LINE),
            P(),
            P("lat", None, GROUP),
            P(None, LINE, None),
            P(LINE, None),
            P(LINE, None),
            P(LINE, None),
            P(LINE),
            P(LINE),
        ),
        out_specs=(P(GROUP, "lat", None), P(None, LINE, None)),
        check_vma=False,
    )
```
